32 devices in a mesh: row: 8 (over z, y), col: 4 (over x, core).
Axes of the slice: x: 2, y: 2, z: 4, core: 2. Of those that a mesh axis runs over, the one named last changes fastest.
Arguments:
- grid_values: bfloat16 [128, 256, 384], P(('row', 'col')), may hold values from -0.21875 to 0.21875
- external: float32 [128, 256], P(('row', 'col')), may hold values from 0 to 6
- tiles: int32 [128, 3], P(('row', 'col')), may hold values from 0 to 31, as said below
- kinetic: bfloat16 [16384, 16384], P('row', 'col'), may hold values from -0.046875 to 0.046875
- orbitals: bfloat16 [16384, 256], P(('row', 'col')), may hold values from -6 to 6
Outputs:
- filtered: float32 [16384, 256], P(('row', 'col'))
The draws below stay inside these ranges and needn't reach their ends.
Inputs may be any that keep to these rules, and one draw needn't show every extreme that they name: Each batch names 3 distinct tiles in increasing order. Among the 4 batches of one device no tile is named more than 2 times; in every draw some tile is named exactly 2 times by the batches of every device.
All inputs are finite; a program needn't handle non-finite values.
Results may differ from the reference program's by a relative error of at most 0.0064.
Values may be sent and summed in bfloat16 or wider, within the bound.
No kernel may reach another device: no remote copies, remote signals or barrier semaphores. Data moves between devices by JAX's collectives and lax.ppermute only.
A program may use at most 128 MiB of HBM per device.

```python
import jax
import jax.numpy as jnp
from jax import lax

NB = 16384
NORB = 256
TILE = 128
LISTED = 3
CAP = 2
B_DEV = 4
PTS = 256
LIST = 384
BATCHES = 128
TPC = 32
TILE_HITS = 3
N_ROW = 8
N_COL = 4
DEVICES = 32


def draw_tiles(key, part):
    tickets = TPC * CAP
    favored = jax.random.randint(jax.random.fold_in(key, 7), (), 0, TPC)

    def one_device(device_key):
        drawn = jax.random.randint(device_key, (tickets,), 0, tickets)
        ticket_ids = jnp.arange(tickets, dtype=jnp.int32)
        scores = drawn * tickets + ticket_ids
        scores = jnp.where(ticket_ids // CAP == favored, tickets * tickets + ticket_ids, scores)
        _, chosen = lax.top_k(scores, B_DEV * LISTED)
        chosen = jnp.sort(chosen)
        return (chosen // CAP).reshape(LISTED, B_DEV).T
    device_keys = jax.random.split(jax.random.fold_in(key, 11), DEVICES)
    return jax.vmap(one_device)(device_keys).reshape(DEVICES * B_DEV, LISTED).astype(jnp.int32)


def level_of(stream_key, shape, shards, least, largest):
    factor_of = 1.0
    for position, parts in shards:
        heights = jax.random.uniform(jax.random.fold_in(jax.random.fold_in(stream_key, 6), position), (parts,), jnp.float32, least / len(shards), largest / len(shards))
        factor_of = factor_of * jnp.repeat(jnp.exp(heights), shape[position] // parts).reshape((-1,) + (1,) * (len(shape) - 1 - position))
    return factor_of


def gaussian(rng, dims, deviation, bound, shards=(), held_as=jnp.bfloat16):
    array = jax.random.normal(rng, dims, jnp.float32) * deviation
    if len(shards) > 0:
        array = level_of(rng, dims, shards, -0.22, 0.18) * array
    return jnp.clip(array, min=-bound, max=bound).astype(held_as)


def setup_inputs(seed: int = 0) -> dict:
    key_list = jax.random.split(jax.random.key(seed), 6)
    grid_values = gaussian(key_list[0], (BATCHES, PTS, LIST), (PTS * TILE_HITS) ** -0.5, 0.21875, ((0, 32),))
    external = jnp.clip(6.0 * jax.random.uniform(key_list[1], (BATCHES, PTS), jnp.float32) ** level_of(key_list[1], (BATCHES, PTS), ((0, 32),), -0.2, 0.2), 0.0, 6.0)
    tiles = draw_tiles(jax.random.fold_in(key_list[5], 71), 0)
    kinetic = gaussian(key_list[3], (NB, NB), NB ** -0.5, 0.046875, ((0, 8), (1, 4)))
    orbitals = gaussian(key_list[4], (NB, NORB), 1.0, 6.0, ((0, 32),))
    return dict(grid_values=grid_values, external=external, tiles=tiles, kinetic=kinetic, orbitals=orbitals)


center = 1.0
spread = 2.5


def reference(grid_values, external, tiles, kinetic, orbitals):
    shard_rows = NB // (N_ROW * N_COL)
    per_shard = shard_rows // TILE
    column_group = (jnp.arange(BATCHES, dtype=jnp.int32) // B_DEV) % N_COL
    starts = ((tiles // per_shard) * N_COL + column_group[:, None]) * shard_rows + (tiles % per_shard) * TILE
    listed = (starts[:, :, None] + jnp.arange(TILE, dtype=jnp.int32)[None, None, :]).reshape(BATCHES, LIST).astype(jnp.int32)

    def one_batch(summed_grid, inputs):
        values, outside, index = inputs
        waves = jnp.dot(values, orbitals[index], preferred_element_type=jnp.float32)
        density = jnp.sum(waves * waves, axis=1)
        potential = outside - jnp.cbrt(3.0 * density / jnp.pi)
        weighted = (potential[:, None] * values.astype(jnp.float32)).astype(jnp.bfloat16)
        integral = jnp.dot(values.T, weighted, preferred_element_type=jnp.float32)
        summed_grid = summed_grid.at[index[:, None], index[None, :]].add(integral)
        return summed_grid, None

    grid_matrix, _ = lax.scan(one_batch, jnp.zeros((NB, NB), jnp.float32), (grid_values, external, listed))
    ordered = kinetic.reshape(NB, N_COL, N_ROW, shard_rows).transpose(0, 2, 1, 3).reshape(NB, NB)
    hamiltonian = (ordered.astype(jnp.float32) + grid_matrix).astype(jnp.bfloat16)

    def apply(vectors):
        return jnp.dot(hamiltonian, vectors, preferred_element_type=jnp.float32) / spread - (center / spread) * vectors.astype(jnp.float32)

    filtered_one = apply(orbitals).astype(jnp.bfloat16)
    filtered_two = (2.0 * apply(filtered_one) - orbitals.astype(jnp.float32)).astype(jnp.bfloat16)
    return 2.0 * apply(filtered_two) - filtered_one.astype(jnp.float32)
```

```python
import functools

import jax
import jax.numpy as jnp
from jax import lax
from jax.experimental import pallas as pl
from jax.experimental.pallas import tpu as pltpu
from jax.sharding import PartitionSpec as P

TILE = 128
center = 1.0
spread = 2.5


def own_rows_kernel(listed, per_shard, batches, where_ref, tiles_ref, values_ref, potential_ref, kinetic_ref, out_ref, total):
    batch = pl.program_id(0)

    @pl.when(batch == 0)
    def _():
        total[...] = kinetic_ref[...].astype(jnp.float32)

    first = where_ref[1] * per_shard
    spots = [tiles_ref[batch * listed + i] for i in range(listed)]
    owned = [(s >= first) & (s < first + per_shard) for s in spots]

    @pl.when(functools.reduce(jnp.logical_or, owned))
    def _():
        values = values_ref[0]
        lane = lax.broadcasted_iota(jnp.int32, potential_ref.shape, 1)
        potential = jnp.sum(jnp.where(lane == batch, potential_ref[...], 0.0), axis=1, keepdims=True)
        weighted = (potential * values.astype(jnp.float32)).astype(jnp.bfloat16)
        for i in range(listed):

            @pl.when(owned[i])
            def _(i=i):
                strip = lax.dot_general(
                    values[:, i * TILE : (i + 1) * TILE],
                    weighted,
                    (((0,), (0,)), ((), ())),
                    preferred_element_type=jnp.float32,
                )
                rows = pl.ds(pl.multiple_of((spots[i] - first) * TILE, TILE), TILE)
                for j in range(listed):
                    columns = pl.ds(pl.multiple_of(spots[j] * TILE, TILE), TILE)
                    total[rows, columns] += strip[:, j * TILE : (j + 1) * TILE]

    @pl.when(batch == batches - 1)
    def _():
        out_ref[...] = total[...].astype(jnp.bfloat16)


def own_rows(where, tiles, values, potential, kinetic, shard_rows):
    batches, points, length = values.shape
    listed = length // TILE
    width = kinetic.shape[1]
    return pl.pallas_call(
        functools.partial(own_rows_kernel, listed, shard_rows // TILE, batches),
        out_shape=jax.ShapeDtypeStruct((shard_rows, width), jnp.bfloat16),
        grid_spec=pltpu.PrefetchScalarGridSpec(
            num_scalar_prefetch=2,
            grid=(batches,),
            in_specs=[
                pl.BlockSpec((1, points, length), lambda b, w, t: (b, 0, 0)),
                pl.BlockSpec((points, batches), lambda b, w, t: (0, 0)),
                pl.BlockSpec((shard_rows, width), lambda b, w, t: (w[0], 0)),
            ],
            out_specs=pl.BlockSpec((shard_rows, width), lambda b, w, t: (0, 0)),
            scratch_shapes=[pltpu.VMEM((shard_rows, width), jnp.float32)],
        ),
        compiler_params=pltpu.CompilerParams(vmem_limit_bytes=48 * 2**20),
        cost_estimate=pl.CostEstimate(
            flops=batches * 2 * points * length * TILE,
            bytes_accessed=values.size * 2 + shard_rows * width * 4,
            transcendentals=0,
        ),
    )(where, tiles, values, potential, kinetic)


def product_kernel(where_ref, kinetic_ref, own_ref, vectors_ref, partial_ref, mine_ref):
    block = pl.program_id(0)

    @pl.when(block != where_ref[0])
    def _():
        partial_ref[...] = jnp.dot(
            kinetic_ref[...], vectors_ref[...], preferred_element_type=jnp.float32
        ).astype(jnp.bfloat16)

    @pl.when(block == where_ref[0])
    def _():
        partial_ref[...] = jnp.zeros_like(partial_ref)
        mine_ref[...] = jnp.dot(
            own_ref[...], vectors_ref[...], preferred_element_type=jnp.float32
        )


def product(where, kinetic, own, vectors):
    rows, width = kinetic.shape
    shard_rows, count = own.shape[0], vectors.shape[1]
    return pl.pallas_call(
        product_kernel,
        out_shape=(
            jax.ShapeDtypeStruct((rows, count), jnp.bfloat16),
            jax.ShapeDtypeStruct((shard_rows, count), jnp.float32),
        ),
        grid_spec=pltpu.PrefetchScalarGridSpec(
            num_scalar_prefetch=1,
            grid=(rows // shard_rows,),
            in_specs=[
                pl.BlockSpec((shard_rows, width), lambda b, w: (b, 0)),
                pl.BlockSpec((shard_rows, width), lambda b, w: (0, 0)),
                pl.BlockSpec((width, count), lambda b, w: (0, 0)),
            ],
            out_specs=(
                pl.BlockSpec((shard_rows, count), lambda b, w: (b, 0)),
                pl.BlockSpec((shard_rows, count), lambda b, w: (0, 0)),
            ),
        ),
        compiler_params=pltpu.CompilerParams(vmem_limit_bytes=48 * 2**20),
        cost_estimate=pl.CostEstimate(
            flops=2 * rows * width * count,
            bytes_accessed=(rows + shard_rows) * width * 2 + width * count * 2 + rows * count * 2,
            transcendentals=0,
        ),
    )(where, kinetic, own, vectors)


def body(grid_values, external, tiles, kinetic, orbitals):
    shard_rows, orbital_count = orbitals.shape
    batch_count, points, length = grid_values.shape
    where = jnp.stack([lax.axis_index("col"), lax.axis_index("row")]).astype(jnp.int32)

    def gather(array):
        return lax.all_gather(array, "row", axis=0, tiled=True)

    group_orbitals = gather(orbitals)
    group_values = gather(grid_values)
    group_tiles = gather(tiles)
    listed_orbitals = group_orbitals.reshape(-1, TILE, orbital_count)[tiles].reshape(
        batch_count, length, orbital_count
    )
    waves = jnp.einsum(
        "bpl,blk->bpk", grid_values, listed_orbitals, preferred_element_type=jnp.float32
    )
    density = jnp.sum(waves * waves, axis=2)
    potential = external - jnp.cbrt(3.0 * density / jnp.pi)
    group_potential = gather(potential)
    own = own_rows(
        where, group_tiles.reshape(-1), group_values, group_potential.T, kinetic, shard_rows
    )

    def filter_step(group_vectors, vectors):
        partial, mine = product(where, kinetic, own, group_vectors)
        arrived = lax.all_to_all(
            partial.reshape(-1, shard_rows, orbital_count), "col", split_axis=0, concat_axis=0
        )
        reduced = jnp.sum(arrived.astype(jnp.float32), axis=0) + mine
        return reduced / spread - center / spread * vectors.astype(jnp.float32)

    first_term = filter_step(group_orbitals, orbitals).astype(jnp.bfloat16)
    second_term = (
        2.0 * filter_step(gather(first_term), first_term) - orbitals.astype(jnp.float32)
    ).astype(jnp.bfloat16)
    return 2.0 * filter_step(gather(second_term), second_term) - first_term.astype(jnp.float32)


def solution(mesh):
    return jax.shard_map(
        body,
        mesh=mesh,
        in_specs=(
            P(("row", "col"), None, None),
            P(("row", "col"), None),
            P(("row", "col"), None),
            P("row", "col"),
            P(("row", "col"), None),
        ),
        out_specs=P(("row", "col"), None),
        check_vma=False,
    )
```

```python
import functools

import jax
import jax.numpy as jnp
from jax import lax
from jax.experimental import pallas as pl
from jax.experimental.pallas import tpu as pltpu
from jax.sharding import PartitionSpec as P

TILE = 128
VMEM_LIMIT = 40 * 2**20
center = 1.0
spread = 2.5


def routes(count):
    found, depth = [], {0: 0}

    def add(mask, source, step):
        depth[mask] = depth[source] + 1
        found.append((mask, source, step))

    for k in sorted(range(1, count // 2), key=lambda k: (k & (k + 1)) != 0):
        full = (1 << k.bit_length()) - 1
        add(2 * k, 0 if k == full else 2 * full, 2 * k if k == full else 2 * (full ^ k))
    if count > 1:
        add(1, 0, 1)
    for k in sorted(range(1, count // 2), key=lambda k: (k & (k + 1)) != 0):
        full = (1 << k.bit_length()) - 1
        add(2 * k + 1, 2 * k if k == full else 2 * full + 1, 1 if k == full else 2 * (full ^ k))
    return sorted(found, key=lambda route: depth[route[0]]), depth


def swap(array, axis, mask):
    return lax.ppermute(array, axis, [(i, i ^ mask) for i in range(lax.axis_size(axis))])


def spread_out(array):
    pieces = {0: array}
    for mask, source, step in routes(lax.axis_size("row"))[0]:
        pieces[mask] = swap(pieces[source], "row", step)
    return pieces


def rows_kernel(listed, masks, batches, first_call, last_call, where_ref, tiles_ref, *refs):
    values_refs, (potential_ref, start_ref), (out_ref, total) = (
        refs[: len(masks)],
        refs[len(masks) : len(masks) + 2],
        refs[len(masks) + 2 :],
    )
    target = total if last_call else out_ref
    target[...] = start_ref[...].astype(jnp.float32)
    per_shard = start_ref.shape[0] // TILE
    first = where_ref[1] * per_shard

    for values_ref, mask in zip(values_refs, masks):

        def one_batch(b, carry, values_ref=values_ref, mask=mask):
            number = mask * batches + b
            spots = [tiles_ref[number * listed + i] for i in range(listed)]
            owned = [(s >= first) & (s < first + per_shard) for s in spots]

            @pl.when(functools.reduce(jnp.logical_or, owned))
            def _():
                values = values_ref[b]
                lane = lax.broadcasted_iota(jnp.int32, potential_ref.shape, 1)
                potential = jnp.sum(
                    jnp.where(lane == number, potential_ref[...], 0.0), axis=1, keepdims=True
                )
                weighted = (potential * values.astype(jnp.float32)).astype(jnp.bfloat16)
                for i in range(listed):

                    @pl.when(owned[i])
                    def _(i=i):
                        strip = lax.dot_general(
                            values[:, i * TILE : (i + 1) * TILE],
                            weighted,
                            (((0,), (0,)), ((), ())),
                            preferred_element_type=jnp.float32,
                        )
                        rows = pl.ds(pl.multiple_of((spots[i] - first) * TILE, TILE), TILE)
                        for j in range(listed):
                            columns = pl.ds(pl.multiple_of(spots[j] * TILE, TILE), TILE)
                            target[rows, columns] += strip[:, j * TILE : (j + 1) * TILE]

            return carry

        lax.fori_loop(0, batches, one_batch, 0)
    if last_call:
        out_ref[...] = total[...].astype(jnp.bfloat16)


def add_rows(where, tiles, pieces, masks, potential, start, shard_rows, first_call, last_call):
    batches, points, length = pieces[0].shape
    listed = length // TILE
    width = start.shape[1]
    whole = pl.BlockSpec((batches, points, length), lambda i, w, t: (0, 0, 0))
    return pl.pallas_call(
        functools.partial(rows_kernel, listed, masks, batches, first_call, last_call),
        out_shape=jax.ShapeDtypeStruct((shard_rows, width), jnp.bfloat16 if last_call else jnp.float32),
        grid_spec=pltpu.PrefetchScalarGridSpec(
            num_scalar_prefetch=2,
            grid=(1,),
            in_specs=[whole for _ in masks]
            + [
                pl.BlockSpec(potential.shape, lambda i, w, t: (0, 0)),
                pl.BlockSpec(
                    (shard_rows, width),
                    (lambda i, w, t: (w[0], 0)) if first_call else (lambda i, w, t: (0, 0)),
                ),
            ],
            out_specs=pl.BlockSpec((shard_rows, width), lambda i, w, t: (0, 0)),
            scratch_shapes=[
                pltpu.VMEM((shard_rows, width) if last_call else (8, TILE), jnp.float32)
            ],
        ),
        compiler_params=pltpu.CompilerParams(vmem_limit_bytes=VMEM_LIMIT),
        cost_estimate=pl.CostEstimate(
            flops=len(masks) * batches * 2 * points * length * TILE,
            bytes_accessed=len(masks) * pieces[0].size * 2 + shard_rows * width * 8,
            transcendentals=0,
        ),
    )(where, tiles, *pieces, potential, start)


def early_kernel(count, where_ref, *refs):
    out_ref = refs[-1]
    total = jnp.dot(refs[0][...], refs[count][...], preferred_element_type=jnp.float32)
    for i in range(1, count):
        total += jnp.dot(refs[i][...], refs[count + i][...], preferred_element_type=jnp.float32)
    out_ref[0] = total


def early_product(where, kinetic, pieces, masks, partners):
    shard_rows, count = pieces[0].shape
    return pl.pallas_call(
        functools.partial(early_kernel, len(masks)),
        out_shape=jax.ShapeDtypeStruct((partners, shard_rows, count), jnp.float32),
        grid_spec=pltpu.PrefetchScalarGridSpec(
            num_scalar_prefetch=1,
            grid=(partners,),
            in_specs=[
                pl.BlockSpec(
                    (shard_rows, shard_rows),
                    lambda s, w, mask=mask: (w[0] ^ (s + 1), w[1] ^ mask),
                )
                for mask in masks
            ]
            + [pl.BlockSpec((shard_rows, count), lambda s, w: (0, 0)) for _ in masks],
            out_specs=pl.BlockSpec((1, shard_rows, count), lambda s, w: (s, 0, 0)),
        ),
        compiler_params=pltpu.CompilerParams(vmem_limit_bytes=VMEM_LIMIT),
        cost_estimate=pl.CostEstimate(
            flops=2 * partners * shard_rows * shard_rows * len(masks) * count,
            bytes_accessed=2 * partners * shard_rows * shard_rows * len(masks),
            transcendentals=0,
        ),
    )(where, *[kinetic] * len(masks), *pieces)


def late_kernel(count, where_ref, *refs):
    early_ref, out_ref = refs[-2:]
    total = early_ref[0]
    for i in range(count):
        total += jnp.dot(refs[i][...], refs[count + i][...], preferred_element_type=jnp.float32)
    out_ref[...] = total.astype(jnp.bfloat16)


def late_product(where, kinetic, pieces, masks, early, partner):
    shard_rows, count = pieces[0].shape
    return pl.pallas_call(
        functools.partial(late_kernel, len(masks)),
        out_shape=jax.ShapeDtypeStruct((shard_rows, count), jnp.bfloat16),
        grid_spec=pltpu.PrefetchScalarGridSpec(
            num_scalar_prefetch=1,
            grid=(1,),
            in_specs=[
                pl.BlockSpec(
                    (shard_rows, shard_rows),
                    lambda s, w, mask=mask: (w[0] ^ partner, w[1] ^ mask),
                )
                for mask in masks
            ]
            + [pl.BlockSpec((shard_rows, count), lambda s, w: (0, 0)) for _ in masks]
            + [pl.BlockSpec((1, shard_rows, count), lambda s, w: (partner - 1, 0, 0))],
            out_specs=pl.BlockSpec((shard_rows, count), lambda s, w: (0, 0)),
        ),
        compiler_params=pltpu.CompilerParams(vmem_limit_bytes=VMEM_LIMIT),
        cost_estimate=pl.CostEstimate(
            flops=2 * shard_rows * shard_rows * len(masks) * count,
            bytes_accessed=2 * shard_rows * shard_rows * len(masks),
            transcendentals=0,
        ),
    )(where, *[kinetic] * len(masks), *pieces, early)


def own_kernel(count, where_ref, *refs):
    out_ref = refs[-1]
    total = jnp.dot(refs[0][...], refs[count][...], preferred_element_type=jnp.float32)
    for i in range(1, count):
        total += jnp.dot(refs[i][...], refs[count + i][...], preferred_element_type=jnp.float32)
    out_ref[...] = total


def own_product(where, own, pieces):
    shard_rows, count = pieces[0].shape
    masks = sorted(pieces)
    return pl.pallas_call(
        functools.partial(own_kernel, len(masks)),
        out_shape=jax.ShapeDtypeStruct((shard_rows, count), jnp.float32),
        grid_spec=pltpu.PrefetchScalarGridSpec(
            num_scalar_prefetch=1,
            grid=(1,),
            in_specs=[
                pl.BlockSpec((shard_rows, shard_rows), lambda s, w, mask=mask: (0, w[1] ^ mask))
                for mask in masks
            ]
            + [pl.BlockSpec((shard_rows, count), lambda s, w: (0, 0)) for _ in masks],
            out_specs=pl.BlockSpec((shard_rows, count), lambda s, w: (0, 0)),
        ),
        compiler_params=pltpu.CompilerParams(vmem_limit_bytes=VMEM_LIMIT),
        cost_estimate=pl.CostEstimate(
            flops=2 * shard_rows * shard_rows * len(masks) * count,
            bytes_accessed=2 * shard_rows * shard_rows * len(masks),
            transcendentals=0,
        ),
    )(where, *[own] * len(masks), *[pieces[mask] for mask in masks])


def body(grid_values, external, tiles, kinetic, orbitals):
    shard_rows, orbital_count = orbitals.shape
    batch_count, points, length = grid_values.shape
    row_count, col_count = lax.axis_size("row"), lax.axis_size("col")
    row = lax.axis_index("row")
    per_shard = shard_rows // TILE
    where = jnp.stack([lax.axis_index("col"), row]).astype(jnp.int32)
    order, depth = routes(row_count)
    masks = sorted(depth)
    soon = [mask for mask in masks if depth[mask] <= 1]
    later = [mask for mask in masks if depth[mask] > 1]

    orbital_pieces = spread_out(orbitals)
    grid_values_later, _ = lax.optimization_barrier(
        (grid_values, [orbital_pieces[mask] for mask in masks if depth[mask] <= 2])
    )
    half = batch_count // 2
    value_pieces = [spread_out(grid_values_later[:half]), spread_out(grid_values_later[half:])]

    by_mask = jnp.stack([orbital_pieces[mask] for mask in masks]).reshape(-1, TILE, orbital_count)
    slots = ((tiles // per_shard) ^ row) * per_shard + tiles % per_shard
    listed_orbitals = by_mask[slots].reshape(batch_count, length, orbital_count)
    waves = jnp.einsum(
        "bpl,blk->bpk", grid_values, listed_orbitals, preferred_element_type=jnp.float32
    )
    density = jnp.sum(waves * waves, axis=2)
    potential = external - jnp.cbrt(3.0 * density / jnp.pi)
    notes = jnp.concatenate(
        [potential, jnp.pad(tiles.astype(jnp.float32), ((0, 0), (0, TILE - tiles.shape[1])))], axis=1
    )[None]
    step = 1
    while step < row_count:
        notes = jnp.concatenate([notes, swap(notes, "row", step)], axis=0)
        step *= 2
    group_potential = notes[:, :, :points].reshape(-1, points).T
    group_tiles = notes[:, :, points : points + tiles.shape[1]].astype(jnp.int32)

    def rows_of(part, chosen, start, first_call, last_call):
        return add_rows(
            where,
            group_tiles[:, part * half : (part + 1) * half].reshape(-1),
            [value_pieces[part][mask] for mask in chosen],
            chosen,
            group_potential.reshape(points, row_count, batch_count)[
                :, :, part * half : (part + 1) * half
            ].reshape(points, -1),
            start,
            shard_rows,
            first_call,
            last_call,
        )

    def send(pieces):
        early = early_product(where, kinetic, [pieces[m] for m in soon], soon, col_count - 1)
        arrived = []
        for partner in range(col_count - 1, 0, -1):
            part = late_product(where, kinetic, [pieces[m] for m in later], later, early, partner)
            arrived.append(swap(part, "col", partner))
        return arrived

    def finish(pieces, arrived, vectors):
        reduced = own_product(where, own, pieces)
        for part in arrived:
            reduced = reduced + part.astype(jnp.float32)
        return reduced / spread - center / spread * vectors.astype(jnp.float32)

    arrived = send(orbital_pieces)
    total = rows_of(0, masks, kinetic, True, False)
    own = rows_of(1, masks, total, False, True)
    first_term = finish(orbital_pieces, arrived, orbitals).astype(jnp.bfloat16)
    first_pieces = spread_out(first_term)
    second_term = (
        2.0 * finish(first_pieces, send(first_pieces), first_term) - orbitals.astype(jnp.float32)
    ).astype(jnp.bfloat16)
    second_pieces = spread_out(second_term)
    return 2.0 * finish(second_pieces, send(second_pieces), second_term) - first_term.astype(
        jnp.float32
    )


def solution(mesh):
    return jax.shard_map(
        body,
        mesh=mesh,
        in_specs=(
            P(("row", "col"), None, None),
            P(("row", "col"), None),
            P(("row", "col"), None),
            P("row", "col"),
            P(("row", "col"), None),
        ),
        out_specs=P(("row", "col"), None),
        check_vma=False,
    )
```

```python
import functools

import jax
import jax.numpy as jnp
from jax import lax
from jax.experimental import pallas as pl
from jax.experimental.pallas import tpu as pltpu
from jax.sharding import PartitionSpec as P

TILE = 128
SMALL_LIMIT = 16 * 2**20
ROWS_LIMIT = 30 * 2**20
center = 1.0
spread = 2.5


def routes(count):
    found, depth = [], {0: 0}

    def add(mask, source, step):
        depth[mask] = depth[source] + 1
        found.append((mask, source, step))

    for k in sorted(range(1, count // 2), key=lambda k: (k & (k + 1)) != 0):
        full = (1 << k.bit_length()) - 1
        add(2 * k, 0 if k == full else 2 * full, 2 * k if k == full else 2 * (full ^ k))
    if count > 1:
        add(1, 0, 1)
    for k in sorted(range(1, count // 2), key=lambda k: (k & (k + 1)) != 0):
        full = (1 << k.bit_length()) - 1
        add(2 * k + 1, 2 * k if k == full else 2 * full + 1, 1 if k == full else 2 * (full ^ k))
    return sorted(found, key=lambda route: depth[route[0]]), depth


def swap(array, axis, mask):
    return lax.ppermute(array, axis, [(i, i ^ mask) for i in range(lax.axis_size(axis))])


def spread_out(array, between=None):
    order, depth = routes(lax.axis_size("row"))
    pieces, result = {0: array}, None
    for mask, source, step in order:
        outgoing = pieces[source]
        if between is not None and depth[mask] > 2:
            if result is None:
                result = between(pieces)
            outgoing, result = lax.optimization_barrier((outgoing, result))
        pieces[mask] = swap(outgoing, "row", step)
    if between is None:
        return pieces
    return pieces, between(pieces) if result is None else result


def hop(pieces, hops, after):
    order, depth = routes(lax.axis_size("row"))
    chosen = [route for route in order if depth[route[0]] == hops]
    sources = sorted({source for _, source, _ in chosen})
    held, after = lax.optimization_barrier(([pieces[source] for source in sources], after))
    held = dict(zip(sources, held))
    for mask, source, step in chosen:
        pieces[mask] = swap(held[source], "row", step)
    return after


def noted(orbitals, external, tiles):
    parts, rest = [], external
    for _ in range(3):
        part = lax.reduce_precision(rest, exponent_bits=8, mantissa_bits=7)
        parts.append(part.reshape(-1))
        rest = rest - part
    flat = jnp.concatenate(parts + [tiles.astype(jnp.float32).reshape(-1)])
    count = orbitals.shape[1]
    flat = jnp.pad(flat, (0, -flat.size % (16 * count))).astype(jnp.bfloat16)
    return jnp.concatenate([orbitals, flat.reshape(-1, count)], axis=0)


def stack_kernel(count, *refs):
    held_ref, notes_ref = refs[count:]
    rows = held_ref.shape[1]
    for i in range(count):
        held_ref[i] = refs[i][:rows]
        notes_ref[i] = refs[i][rows:].astype(jnp.float32)


def stacked(pieces, shard_rows):
    masks = sorted(pieces)
    rows, count = pieces[0].shape
    return pl.pallas_call(
        functools.partial(stack_kernel, len(masks)),
        out_shape=(
            jax.ShapeDtypeStruct((len(masks), shard_rows, count), jnp.bfloat16),
            jax.ShapeDtypeStruct((len(masks), rows - shard_rows, count), jnp.float32),
        ),
        compiler_params=pltpu.CompilerParams(vmem_limit_bytes=SMALL_LIMIT),
        cost_estimate=pl.CostEstimate(
            flops=0, bytes_accessed=4 * len(masks) * rows * count, transcendentals=0
        ),
    )(*[pieces[mask] for mask in masks])


def rows_kernel(listed, firsts, last_call, where_ref, tiles_ref, *refs):
    values_refs, (external_ref, held_ref, start_ref), (out_ref, total) = (
        refs[: len(firsts)],
        refs[len(firsts) : len(firsts) + 3],
        refs[len(firsts) + 3 :],
    )
    target = total if last_call else out_ref
    target[...] = start_ref[...].astype(jnp.float32)
    per_shard = start_ref.shape[0] // TILE
    mine = where_ref[1] * per_shard

    for values_ref, first in zip(values_refs, firsts):

        def one_batch(b, carry, values_ref=values_ref, first=first):
            spots = [tiles_ref[(first + b) * listed + i] for i in range(listed)]
            owned = [(s >= mine) & (s < mine + per_shard) for s in spots]

            @pl.when(functools.reduce(jnp.logical_or, owned))
            def _():
                values = values_ref[b]
                waves = None
                for i in range(listed):
                    orbital_rows = pl.ds(pl.multiple_of(spots[i] % per_shard * TILE, TILE), TILE)
                    part = jnp.dot(
                        values[:, i * TILE : (i + 1) * TILE],
                        held_ref[(spots[i] // per_shard) ^ where_ref[1], orbital_rows, :],
                        preferred_element_type=jnp.float32,
                    )
                    waves = part if waves is None else waves + part
                lifted = jnp.sum(waves * waves, axis=1, keepdims=True) * (3.0 / jnp.pi)
                root = jnp.where(lifted > 0.0, jnp.exp(jnp.log(lifted) * (1.0 / 3.0)), 0.0)
                lane = lax.broadcasted_iota(jnp.int32, external_ref.shape, 1)
                external = jnp.sum(
                    jnp.where(lane == first + b, external_ref[...], 0.0), axis=1, keepdims=True
                )
                potential = external - root
                weighted = (potential * values.astype(jnp.float32)).astype(jnp.bfloat16)
                for i in range(listed):

                    @pl.when(owned[i])
                    def _(i=i):
                        strip = lax.dot_general(
                            values[:, i * TILE : (i + 1) * TILE],
                            weighted,
                            (((0,), (0,)), ((), ())),
                            preferred_element_type=jnp.float32,
                        )
                        rows = pl.ds(pl.multiple_of((spots[i] - mine) * TILE, TILE), TILE)
                        for j in range(listed):
                            columns = pl.ds(pl.multiple_of(spots[j] * TILE, TILE), TILE)
                            target[rows, columns] += strip[:, j * TILE : (j + 1) * TILE]

            return carry

        lax.fori_loop(0, values_ref.shape[0], one_batch, 0)
    if last_call:
        out_ref[...] = total[...].astype(jnp.bfloat16)


def add_rows(
    where, tiles, pieces, firsts, external, held, start, shard_rows, first_call, last_call
):
    batches, points, length = pieces[0].shape
    listed = length // TILE
    width = start.shape[1]
    once = pl.Buffered(1)
    whole = pl.BlockSpec(
        (batches, points, length), lambda i, w, t: (0, 0, 0), pipeline_mode=once
    )
    return pl.pallas_call(
        functools.partial(rows_kernel, listed, firsts, last_call),
        out_shape=jax.ShapeDtypeStruct((shard_rows, width), jnp.bfloat16 if last_call else jnp.float32),
        grid_spec=pltpu.PrefetchScalarGridSpec(
            num_scalar_prefetch=2,
            grid=(1,),
            in_specs=[whole for _ in firsts]
            + [
                pl.BlockSpec(external.shape, lambda i, w, t: (0, 0)),
                pl.BlockSpec(held.shape, lambda i, w, t: (0, 0, 0), pipeline_mode=once),
                pl.BlockSpec(
                    (shard_rows, width),
                    (lambda i, w, t: (w[0], 0)) if first_call else (lambda i, w, t: (0, 0)),
                    pipeline_mode=once,
                ),
            ],
            out_specs=pl.BlockSpec((shard_rows, width), lambda i, w, t: (0, 0), pipeline_mode=once),
            scratch_shapes=[
                pltpu.VMEM((shard_rows, width) if last_call else (8, TILE), jnp.float32)
            ],
        ),
        compiler_params=pltpu.CompilerParams(vmem_limit_bytes=ROWS_LIMIT),
        cost_estimate=pl.CostEstimate(
            flops=len(firsts) * batches * 2 * points * length * TILE,
            bytes_accessed=len(firsts) * pieces[0].size * 2 + shard_rows * width * 8,
            transcendentals=0,
        ),
    )(where, tiles, *pieces, external, held, start)


def early_kernel(count, where_ref, *refs):
    out_ref = refs[-1]
    total = jnp.dot(refs[0][...], refs[count][...], preferred_element_type=jnp.float32)
    for i in range(1, count):
        total += jnp.dot(refs[i][...], refs[count + i][...], preferred_element_type=jnp.float32)
    if len(refs) > 2 * count + 1:
        total += refs[2 * count][0]
    out_ref[0] = total


def early_product(where, kinetic, pieces, masks, partners, before=None):
    shard_rows, count = kinetic.shape[0] // (partners + 1), pieces[0].shape[1]
    whole = pl.BlockSpec((1, shard_rows, count), lambda s, w: (s, 0, 0))
    return pl.pallas_call(
        functools.partial(early_kernel, len(masks)),
        out_shape=jax.ShapeDtypeStruct((partners, shard_rows, count), jnp.float32),
        grid_spec=pltpu.PrefetchScalarGridSpec(
            num_scalar_prefetch=1,
            grid=(partners,),
            in_specs=[
                pl.BlockSpec(
                    (shard_rows, shard_rows),
                    lambda s, w, mask=mask: (w[0] ^ (s + 1), w[1] ^ mask),
                )
                for mask in masks
            ]
            + [pl.BlockSpec((shard_rows, count), lambda s, w: (0, 0)) for _ in masks]
            + [whole] * (before is not None),
            out_specs=whole,
        ),
        compiler_params=pltpu.CompilerParams(vmem_limit_bytes=SMALL_LIMIT),
        cost_estimate=pl.CostEstimate(
            flops=2 * partners * shard_rows * shard_rows * len(masks) * count,
            bytes_accessed=2 * partners * shard_rows * shard_rows * len(masks),
            transcendentals=0,
        ),
    )(where, *[kinetic] * len(masks), *pieces, *([] if before is None else [before]))


def late_kernel(count, where_ref, *refs):
    early_ref, out_ref = refs[-2:]
    total = early_ref[0]
    for i in range(count):
        total += jnp.dot(refs[i][...], refs[count + i][...], preferred_element_type=jnp.float32)
    out_ref[...] = total.astype(jnp.bfloat16)


def late_product(where, kinetic, pieces, masks, early, partner):
    shard_rows, count = early.shape[1:]
    return pl.pallas_call(
        functools.partial(late_kernel, len(masks)),
        out_shape=jax.ShapeDtypeStruct((shard_rows, count), jnp.bfloat16),
        grid_spec=pltpu.PrefetchScalarGridSpec(
            num_scalar_prefetch=1,
            grid=(1,),
            in_specs=[
                pl.BlockSpec(
                    (shard_rows, shard_rows),
                    lambda s, w, mask=mask: (w[0] ^ partner, w[1] ^ mask),
                )
                for mask in masks
            ]
            + [pl.BlockSpec((shard_rows, count), lambda s, w: (0, 0)) for _ in masks]
            + [pl.BlockSpec((1, shard_rows, count), lambda s, w: (partner - 1, 0, 0))],
            out_specs=pl.BlockSpec((shard_rows, count), lambda s, w: (0, 0)),
        ),
        compiler_params=pltpu.CompilerParams(vmem_limit_bytes=SMALL_LIMIT),
        cost_estimate=pl.CostEstimate(
            flops=2 * shard_rows * shard_rows * len(masks) * count,
            bytes_accessed=2 * shard_rows * shard_rows * len(masks),
            transcendentals=0,
        ),
    )(where, *[kinetic] * len(masks), *pieces, early)


def own_kernel(count, where_ref, *refs):
    out_ref = refs[-1]
    total = jnp.dot(refs[0][...], refs[count][...], preferred_element_type=jnp.float32)
    for i in range(1, count):
        total += jnp.dot(refs[i][...], refs[count + i][...], preferred_element_type=jnp.float32)
    out_ref[...] = total


def own_product(where, own, pieces):
    shard_rows, count = own.shape[0], pieces[0].shape[1]
    masks = sorted(pieces)
    return pl.pallas_call(
        functools.partial(own_kernel, len(masks)),
        out_shape=jax.ShapeDtypeStruct((shard_rows, count), jnp.float32),
        grid_spec=pltpu.PrefetchScalarGridSpec(
            num_scalar_prefetch=1,
            grid=(1,),
            in_specs=[
                pl.BlockSpec((shard_rows, shard_rows), lambda s, w, mask=mask: (0, w[1] ^ mask))
                for mask in masks
            ]
            + [pl.BlockSpec((shard_rows, count), lambda s, w: (0, 0)) for _ in masks],
            out_specs=pl.BlockSpec((shard_rows, count), lambda s, w: (0, 0)),
        ),
        compiler_params=pltpu.CompilerParams(vmem_limit_bytes=SMALL_LIMIT),
        cost_estimate=pl.CostEstimate(
            flops=2 * shard_rows * shard_rows * len(masks) * count,
            bytes_accessed=2 * shard_rows * shard_rows * len(masks),
            transcendentals=0,
        ),
    )(where, *[own] * len(masks), *[pieces[mask] for mask in masks])


def body(grid_values, external, tiles, kinetic, orbitals):
    shard_rows, orbital_count = orbitals.shape
    batch_count, points, length = grid_values.shape
    row_count, col_count = lax.axis_size("row"), lax.axis_size("col")
    row = lax.axis_index("row")
    per_shard = shard_rows // TILE
    where = jnp.stack([lax.axis_index("col"), row]).astype(jnp.int32)
    _, depth = routes(row_count)
    masks = sorted(depth)
    soon = [mask for mask in masks if depth[mask] <= 1]
    middle = [mask for mask in masks if depth[mask] == 2]
    last = [mask for mask in masks if depth[mask] > 2]

    def first_products(pieces):
        return early_product(where, kinetic, [pieces[m] for m in soon], soon, col_count - 1)

    def send(pieces, early):
        early = early_product(
            where, kinetic, [pieces[m] for m in middle], middle, col_count - 1, early
        )
        arrived = []
        for partner in range(col_count - 1, 0, -1):
            part = late_product(where, kinetic, [pieces[m] for m in last], last, early, partner)
            arrived.append(swap(part, "col", partner))
        return arrived

    orbital_pieces = spread_out(noted(orbitals, external, tiles))
    held, notes = stacked(orbital_pieces, shard_rows)
    notes = notes.reshape(row_count, -1)
    group_external = (
        notes[:, : external.size]
        + notes[:, external.size : 2 * external.size]
        + notes[:, 2 * external.size : 3 * external.size]
    )
    group_external = group_external.reshape(-1, points).T
    group_tiles = notes[:, 3 * external.size : 3 * external.size + tiles.size]
    group_tiles = group_tiles.astype(jnp.int32).reshape(-1)

    half = batch_count // 2

    def rows_of(chosen, start, first_call, last_call):
        return add_rows(
            where,
            group_tiles,
            [value_pieces[part][mask] for mask, part in chosen],
            [mask * batch_count + part * half for mask, part in chosen],
            group_external,
            held,
            start,
            shard_rows,
            first_call,
            last_call,
        )

    def finish(pieces, arrived, vectors):
        reduced = own_product(where, own, pieces)
        for part in arrived:
            reduced = reduced + part.astype(jnp.float32)
        return reduced / spread - center / spread * vectors.astype(jnp.float32)

    arrived = send(orbital_pieces, first_products(orbital_pieces))
    value_pieces = [{0: grid_values[:half]}, {0: grid_values[half:]}]
    most = max(depth.values())
    taken, total = [], kinetic

    def arrived_values():
        return [(m, p) for p in range(2) for m in sorted(value_pieces[p])]

    for turn in range(1, most + 2):
        after = [orbital_pieces, [value_pieces[p][m] for m, p in arrived_values()]]
        if turn == most:
            taken = arrived_values()
            total = rows_of(taken, kinetic, True, False)
        if turn == most + 1:
            after, total = lax.optimization_barrier((after, total))
        if turn <= most:
            after = hop(value_pieces[0], turn, after)
        if turn > 1:
            hop(value_pieces[1], turn - 1, after)
    rest = [(m, p) for p in range(2) for m in masks if (m, p) not in taken]
    own = rows_of(rest, total, False, True)
    first_term = finish(orbital_pieces, arrived, orbitals).astype(jnp.bfloat16)
    first_pieces, early = spread_out(first_term, first_products)
    second_term = (
        2.0 * finish(first_pieces, send(first_pieces, early), first_term)
        - orbitals.astype(jnp.float32)
    ).astype(jnp.bfloat16)
    second_pieces, early = spread_out(second_term, first_products)
    return 2.0 * finish(second_pieces, send(second_pieces, early), second_term) - first_term.astype(
        jnp.float32
    )


def solution(mesh):
    return jax.shard_map(
        body,
        mesh=mesh,
        in_specs=(
            P(("row", "col"), None, None),
            P(("row", "col"), None),
            P(("row", "col"), None),
            P("row", "col"),
            P(("row", "col"), None),
        ),
        out_specs=P(("row", "col"), None),
        check_vma=False,
    )
```

```python
import functools

import jax
import jax.numpy as jnp
from jax import lax
from jax.experimental import pallas as pl
from jax.experimental.pallas import tpu as pltpu
from jax.sharding import PartitionSpec as P

TILE = 128
SMALL_LIMIT = 18 * 2**20
LARGE_LIMIT = 46 * 2**20
center = 1.0
spread = 2.5


def routes(count):
    found, depth = [], {0: 0}

    def add(mask, source, step):
        depth[mask] = depth[source] + 1
        found.append((mask, source, step))

    for k in sorted(range(1, count // 2), key=lambda k: (k & (k + 1)) != 0):
        full = (1 << k.bit_length()) - 1
        add(2 * k, 0 if k == full else 2 * full, 2 * k if k == full else 2 * (full ^ k))
    if count > 1:
        add(1, 0, 1)
    for k in sorted(range(1, count // 2), key=lambda k: (k & (k + 1)) != 0):
        full = (1 << k.bit_length()) - 1
        add(2 * k + 1, 2 * k if k == full else 2 * full + 1, 1 if k == full else 2 * (full ^ k))
    return sorted(found, key=lambda route: depth[route[0]]), depth


def swap(array, axis, mask):
    return lax.ppermute(array, axis, [(i, i ^ mask) for i in range(lax.axis_size(axis))])


def spread_out(array, between=None):
    order, depth = routes(lax.axis_size("row"))
    pieces, result = {0: array}, None
    for mask, source, step in order:
        outgoing = pieces[source]
        if between is not None and depth[mask] > 2:
            if result is None:
                result = between(pieces)
            outgoing, result = lax.optimization_barrier((outgoing, result))
        pieces[mask] = swap(outgoing, "row", step)
    if between is None:
        return pieces
    return pieces, between(pieces) if result is None else result


def hop(pieces, hops, after):
    order, depth = routes(lax.axis_size("row"))
    held, after = lax.optimization_barrier((dict(pieces), after))
    pieces.update(held)
    for mask, source, step in order:
        if depth[mask] == hops:
            pieces[mask] = swap(pieces[source], "row", step)
    return after


def noted(orbitals, external, tiles):
    parts, rest = [], external
    for _ in range(3):
        part = lax.reduce_precision(rest, exponent_bits=8, mantissa_bits=7)
        parts.append(part.reshape(-1))
        rest = rest - part
    flat = jnp.concatenate(parts + [tiles.astype(jnp.float32).reshape(-1)])
    count = orbitals.shape[1]
    flat = jnp.pad(flat, (0, -flat.size % (16 * count))).astype(jnp.bfloat16)
    return jnp.concatenate([orbitals, flat.reshape(-1, count)], axis=0)


def stack_kernel(count, *refs):
    held_ref, notes_ref = refs[count:]
    rows = held_ref.shape[1]
    for i in range(count):
        held_ref[i] = refs[i][:rows]
        notes_ref[i] = refs[i][rows:].astype(jnp.float32)


def stacked(pieces, shard_rows):
    masks = sorted(pieces)
    rows, count = pieces[0].shape
    return pl.pallas_call(
        functools.partial(stack_kernel, len(masks)),
        out_shape=(
            jax.ShapeDtypeStruct((len(masks), shard_rows, count), jnp.bfloat16),
            jax.ShapeDtypeStruct((len(masks), rows - shard_rows, count), jnp.float32),
        ),
        compiler_params=pltpu.CompilerParams(vmem_limit_bytes=SMALL_LIMIT),
        cost_estimate=pl.CostEstimate(
            flops=0, bytes_accessed=4 * len(masks) * rows * count, transcendentals=0
        ),
    )(*[pieces[mask] for mask in masks])


def rows_kernel(listed, per_shard, firsts, last_call, where_ref, tiles_ref, *refs):
    values_refs, (external_ref, held_ref, start_ref), (out_ref, total) = (
        refs[: len(firsts)],
        refs[len(firsts) : len(firsts) + 3],
        refs[len(firsts) + 3 :],
    )
    target = total if last_call else out_ref
    target[...] = start_ref[...].astype(jnp.float32)
    mine = where_ref[1] * per_shard + pl.program_id(0)

    for values_ref, first in zip(values_refs, firsts):

        def one_batch(b, carry, values_ref=values_ref, first=first):
            spots = [tiles_ref[(first + b) * listed + i] for i in range(listed)]
            owned = [s == mine for s in spots]

            @pl.when(functools.reduce(jnp.logical_or, owned))
            def _():
                values = values_ref[b]
                waves = None
                for i in range(listed):
                    orbital_rows = pl.ds(pl.multiple_of(spots[i] % per_shard * TILE, TILE), TILE)
                    part = jnp.dot(
                        values[:, i * TILE : (i + 1) * TILE],
                        held_ref[(spots[i] // per_shard) ^ where_ref[1], orbital_rows, :],
                        preferred_element_type=jnp.float32,
                    )
                    waves = part if waves is None else waves + part
                lifted = jnp.sum(waves * waves, axis=1, keepdims=True) * (3.0 / jnp.pi)
                root = jnp.where(lifted > 0.0, jnp.exp(jnp.log(lifted) * (1.0 / 3.0)), 0.0)
                lane = lax.broadcasted_iota(jnp.int32, external_ref.shape, 1)
                external = jnp.sum(
                    jnp.where(lane == first + b, external_ref[...], 0.0), axis=1, keepdims=True
                )
                potential = external - root
                weighted = (potential * values.astype(jnp.float32)).astype(jnp.bfloat16)
                place = sum(jnp.where(o, i, 0) for i, o in enumerate(owned))
                strip = lax.dot_general(
                    values_ref[b, :, pl.ds(pl.multiple_of(place * TILE, TILE), TILE)],
                    weighted,
                    (((0,), (0,)), ((), ())),
                    preferred_element_type=jnp.float32,
                )
                for j in range(listed):
                    columns = pl.ds(pl.multiple_of(spots[j] * TILE, TILE), TILE)
                    target[:, columns] += strip[:, j * TILE : (j + 1) * TILE]

            return carry

        lax.fori_loop(0, values_ref.shape[0], one_batch, 0)
    if last_call:
        out_ref[...] = total[...].astype(jnp.bfloat16)


def add_rows(where, tiles, pieces, firsts, external, held, start, last_call):
    batches, points, length = pieces[0].shape
    listed = length // TILE
    shard_rows, width = start.shape
    once = pl.Buffered(1)
    whole = pl.BlockSpec(
        (batches, points, length), lambda i, w, t: (0, 0, 0), pipeline_mode=once
    )
    rows = pl.BlockSpec((TILE, width), lambda i, w, t: (i, 0))
    return pl.pallas_call(
        functools.partial(rows_kernel, listed, shard_rows // TILE, firsts, last_call),
        out_shape=jax.ShapeDtypeStruct(start.shape, jnp.bfloat16 if last_call else jnp.float32),
        grid_spec=pltpu.PrefetchScalarGridSpec(
            num_scalar_prefetch=2,
            grid=(shard_rows // TILE,),
            in_specs=[whole for _ in firsts]
            + [
                pl.BlockSpec(external.shape, lambda i, w, t: (0, 0)),
                pl.BlockSpec(held.shape, lambda i, w, t: (0, 0, 0), pipeline_mode=once),
                rows,
            ],
            out_specs=rows,
            scratch_shapes=[pltpu.VMEM((TILE, width) if last_call else (8, TILE), jnp.float32)],
        ),
        compiler_params=pltpu.CompilerParams(vmem_limit_bytes=SMALL_LIMIT),
        cost_estimate=pl.CostEstimate(
            flops=len(firsts) * batches * 2 * points * length * TILE,
            bytes_accessed=2 * len(firsts) * batches * points * length + shard_rows * width * 8,
            transcendentals=0,
        ),
    )(where, tiles, *pieces, external, held, start)


def early_kernel(count, where_ref, *refs):
    out_ref = refs[-1]
    total = jnp.dot(refs[0][...], refs[count][...], preferred_element_type=jnp.float32)
    for i in range(1, count):
        total += jnp.dot(refs[i][...], refs[count + i][...], preferred_element_type=jnp.float32)
    if len(refs) > 2 * count + 1:
        total += refs[2 * count][0]
    out_ref[0] = total


def early_product(where, kinetic, pieces, masks, partners, limit, before=None):
    shard_rows, count = kinetic.shape[0] // (partners + 1), pieces[0].shape[1]
    whole = pl.BlockSpec((1, shard_rows, count), lambda s, w: (s, 0, 0))
    return pl.pallas_call(
        functools.partial(early_kernel, len(masks)),
        out_shape=jax.ShapeDtypeStruct((partners, shard_rows, count), jnp.float32),
        grid_spec=pltpu.PrefetchScalarGridSpec(
            num_scalar_prefetch=1,
            grid=(partners,),
            in_specs=[
                pl.BlockSpec(
                    (shard_rows, shard_rows),
                    lambda s, w, mask=mask: (w[0] ^ (s + 1), w[1] ^ mask),
                )
                for mask in masks
            ]
            + [pl.BlockSpec((shard_rows, count), lambda s, w: (0, 0)) for _ in masks]
            + [whole] * (before is not None),
            out_specs=whole,
        ),
        compiler_params=pltpu.CompilerParams(vmem_limit_bytes=limit),
        cost_estimate=pl.CostEstimate(
            flops=2 * partners * shard_rows * shard_rows * len(masks) * count,
            bytes_accessed=2 * partners * shard_rows * shard_rows * len(masks),
            transcendentals=0,
        ),
    )(where, *[kinetic] * len(masks), *pieces, *([] if before is None else [before]))


def late_kernel(count, where_ref, *refs):
    early_ref, out_ref = refs[-2:]
    total = early_ref[0]
    for i in range(count):
        total += jnp.dot(refs[i][...], refs[count + i][...], preferred_element_type=jnp.float32)
    out_ref[...] = total.astype(jnp.bfloat16)


def late_product(where, kinetic, pieces, masks, early, partner, limit):
    shard_rows, count = early.shape[1:]
    return pl.pallas_call(
        functools.partial(late_kernel, len(masks)),
        out_shape=jax.ShapeDtypeStruct((shard_rows, count), jnp.bfloat16),
        grid_spec=pltpu.PrefetchScalarGridSpec(
            num_scalar_prefetch=1,
            grid=(1,),
            in_specs=[
                pl.BlockSpec(
                    (shard_rows, shard_rows),
                    lambda s, w, mask=mask: (w[0] ^ partner, w[1] ^ mask),
                )
                for mask in masks
            ]
            + [pl.BlockSpec((shard_rows, count), lambda s, w: (0, 0)) for _ in masks]
            + [pl.BlockSpec((1, shard_rows, count), lambda s, w: (partner - 1, 0, 0))],
            out_specs=pl.BlockSpec((shard_rows, count), lambda s, w: (0, 0)),
        ),
        compiler_params=pltpu.CompilerParams(vmem_limit_bytes=limit),
        cost_estimate=pl.CostEstimate(
            flops=2 * shard_rows * shard_rows * len(masks) * count,
            bytes_accessed=2 * shard_rows * shard_rows * len(masks),
            transcendentals=0,
        ),
    )(where, *[kinetic] * len(masks), *pieces, early)


def own_kernel(count, where_ref, *refs):
    out_ref = refs[-1]
    total = jnp.dot(refs[0][...], refs[count][...], preferred_element_type=jnp.float32)
    for i in range(1, count):
        total += jnp.dot(refs[i][...], refs[count + i][...], preferred_element_type=jnp.float32)
    out_ref[...] = total


def own_product(where, own, pieces):
    shard_rows, count = own.shape[0], pieces[0].shape[1]
    masks = sorted(pieces)
    return pl.pallas_call(
        functools.partial(own_kernel, len(masks)),
        out_shape=jax.ShapeDtypeStruct((shard_rows, count), jnp.float32),
        grid_spec=pltpu.PrefetchScalarGridSpec(
            num_scalar_prefetch=1,
            grid=(1,),
            in_specs=[
                pl.BlockSpec((shard_rows, shard_rows), lambda s, w, mask=mask: (0, w[1] ^ mask))
                for mask in masks
            ]
            + [pl.BlockSpec((shard_rows, count), lambda s, w: (0, 0)) for _ in masks],
            out_specs=pl.BlockSpec((shard_rows, count), lambda s, w: (0, 0)),
        ),
        compiler_params=pltpu.CompilerParams(vmem_limit_bytes=SMALL_LIMIT),
        cost_estimate=pl.CostEstimate(
            flops=2 * shard_rows * shard_rows * len(masks) * count,
            bytes_accessed=2 * shard_rows * shard_rows * len(masks),
            transcendentals=0,
        ),
    )(where, *[own] * len(masks), *[pieces[mask] for mask in masks])


def body(grid_values, external, tiles, kinetic, orbitals):
    shard_rows, orbital_count = orbitals.shape
    batch_count, points, length = grid_values.shape
    row_count, col_count = lax.axis_size("row"), lax.axis_size("col")
    row = lax.axis_index("row")
    per_shard = shard_rows // TILE
    where = jnp.stack([lax.axis_index("col"), row]).astype(jnp.int32)
    _, depth = routes(row_count)
    masks = sorted(depth)
    soon = [mask for mask in masks if depth[mask] <= 1]
    middle = [mask for mask in masks if depth[mask] == 2]
    last = [mask for mask in masks if depth[mask] > 2]

    def first_products(pieces, limit=SMALL_LIMIT):
        return early_product(where, kinetic, [pieces[m] for m in soon], soon, col_count - 1, limit)

    def sums(pieces, early, limit=SMALL_LIMIT):
        early = early_product(
            where, kinetic, [pieces[m] for m in middle], middle, col_count - 1, limit, early
        )
        return [
            late_product(where, kinetic, [pieces[m] for m in last], last, early, partner, limit)
            for partner in range(col_count - 1, 0, -1)
        ]

    def send(parts):
        return [swap(part, "col", len(parts) - i) for i, part in enumerate(parts)]

    orbital_pieces = spread_out(noted(orbitals, external, tiles))
    held, notes = stacked(orbital_pieces, shard_rows)
    notes = notes.reshape(row_count, -1)
    group_external = (
        notes[:, : external.size]
        + notes[:, external.size : 2 * external.size]
        + notes[:, 2 * external.size : 3 * external.size]
    )
    group_external = group_external.reshape(-1, points).T
    group_tiles = notes[:, 3 * external.size : 3 * external.size + tiles.size]
    group_tiles = group_tiles.astype(jnp.int32).reshape(-1)

    half = batch_count // 2

    def rows_of(chosen, start, last_call):
        return add_rows(
            where,
            group_tiles,
            [value_pieces[part][mask] for mask, part in chosen],
            [mask * batch_count + part * half for mask, part in chosen],
            group_external,
            held,
            start,
            last_call,
        )

    def finish(pieces, arrived, vectors):
        reduced = own_product(where, own, pieces)
        for part in arrived:
            reduced = reduced + part.astype(jnp.float32)
        return reduced / spread - center / spread * vectors.astype(jnp.float32)

    value_pieces = [{0: grid_values[:half]}, {0: grid_values[half:]}]
    parts = sums(orbital_pieces, first_products(orbital_pieces, LARGE_LIMIT), LARGE_LIMIT)
    own_kinetic = lax.dynamic_slice_in_dim(kinetic, where[0] * shard_rows, shard_rows, 0)
    most = max(depth.values())
    taken, total = [], own_kinetic

    def arrived_values():
        return [(m, p) for p in range(2) for m in sorted(value_pieces[p])]

    orbital_pieces = hop(value_pieces[0], 1, orbital_pieces)
    for turn in range(2, most + 2):
        fresh = [which for which in arrived_values() if which not in taken]
        taken = taken + fresh
        if turn == most + 1:
            total = hop(value_pieces[1], turn - 1, total)
        else:
            value_pieces[1], parts, total = hop(
                value_pieces[0], turn, (value_pieces[1], parts, total)
            )
            total = hop(value_pieces[1], turn - 1, total)
        if turn <= most:
            total = rows_of(fresh, total, False)
        else:
            taken = [which for which in taken if which not in fresh]
    arrived = send(parts)
    arrived = send(parts)
    rest = [(m, p) for p in range(2) for m in masks if (m, p) not in taken]
    own = rows_of(rest, total, True)
    first_term = finish(orbital_pieces, arrived, orbitals).astype(jnp.bfloat16)
    first_pieces, early = spread_out(first_term, first_products)
    second_term = (
        2.0 * finish(first_pieces, send(sums(first_pieces, early)), first_term)
        - orbitals.astype(jnp.float32)
    ).astype(jnp.bfloat16)
    second_pieces, early = spread_out(second_term, first_products)
    return 2.0 * finish(second_pieces, send(sums(second_pieces, early)), second_term) - first_term.astype(
        jnp.float32
    )


def solution(mesh):
    return jax.shard_map(
        body,
        mesh=mesh,
        in_specs=(
            P(("row", "col"), None, None),
            P(("row", "col"), None),
            P(("row", "col"), None),
            P("row", "col"),
            P(("row", "col"), None),
        ),
        out_specs=P(("row", "col"), None),
        check_vma=False,
    )
```

```python
import functools

import jax
import jax.numpy as jnp
from jax import lax
from jax.experimental import pallas as pl
from jax.experimental.pallas import tpu as pltpu
from jax.sharding import PartitionSpec as P

TILE = 128
SMALL_LIMIT = 18 * 2**20
LARGE_LIMIT = 46 * 2**20
center = 1.0
spread = 2.5


def routes(count):
    found, depth = [], {0: 0}

    def add(mask, source, step):
        depth[mask] = depth[source] + 1
        found.append((mask, source, step))

    for k in sorted(range(1, count // 2), key=lambda k: (k & (k + 1)) != 0):
        full = (1 << k.bit_length()) - 1
        add(2 * k, 0 if k == full else 2 * full, 2 * k if k == full else 2 * (full ^ k))
    if count > 1:
        add(1, 0, 1)
    for k in sorted(range(1, count // 2), key=lambda k: (k & (k + 1)) != 0):
        full = (1 << k.bit_length()) - 1
        add(2 * k + 1, 2 * k if k == full else 2 * full + 1, 1 if k == full else 2 * (full ^ k))
    return sorted(found, key=lambda route: depth[route[0]]), depth


def swap(array, axis, mask):
    return lax.ppermute(array, axis, [(i, i ^ mask) for i in range(lax.axis_size(axis))])


def spread_out(array, between=None):
    order, depth = routes(lax.axis_size("row"))
    pieces, result = {0: array}, None
    for mask, source, step in order:
        outgoing = pieces[source]
        if between is not None and depth[mask] > 2:
            if result is None:
                result = between(pieces)
            outgoing, result = lax.optimization_barrier((outgoing, result))
        pieces[mask] = swap(outgoing, "row", step)
    if between is None:
        return pieces
    return pieces, between(pieces) if result is None else result


def hop(pieces, chosen, after):
    held, after = lax.optimization_barrier((dict(pieces), after))
    pieces.update(held)
    for mask, source, step in chosen:
        pieces[mask] = swap(pieces[source], "row", step)
    return after


def turns(count):
    order, _ = routes(count)
    near = [route for route in order if route[0] % 2 == 0 and route[1] == 0]
    side = [route for route in order if route[0] == 1]
    near_side = [(mask + 1, mask, 1) for mask, _, _ in near]
    far = [route for route in order if route[0] % 2 == 0 and route[1] != 0]
    far_side = [route for route in order if route[0] - 1 in [mask for mask, _, _ in far]]
    last_side = [(mask + 1, mask, 1) for mask, _, _ in far]
    return [near + side, near_side, far, far_side], [side, near, near_side + far, last_side]


def noted(orbitals, external, tiles):
    parts, rest = [], external
    for _ in range(3):
        part = lax.reduce_precision(rest, exponent_bits=8, mantissa_bits=7)
        parts.append(part.reshape(-1))
        rest = rest - part
    flat = jnp.concatenate(parts + [tiles.astype(jnp.float32).reshape(-1)])
    count = orbitals.shape[1]
    flat = jnp.pad(flat, (0, -flat.size % (16 * count))).astype(jnp.bfloat16)
    return jnp.concatenate([orbitals, flat.reshape(-1, count)], axis=0)


def stack_kernel(count, *refs):
    held_ref, notes_ref = refs[count:]
    rows = held_ref.shape[1]
    for i in range(count):
        held_ref[i] = refs[i][:rows]
        notes_ref[i] = refs[i][rows:].astype(jnp.float32)


def stacked(pieces, shard_rows):
    masks = sorted(pieces)
    rows, count = pieces[0].shape
    return pl.pallas_call(
        functools.partial(stack_kernel, len(masks)),
        out_shape=(
            jax.ShapeDtypeStruct((len(masks), shard_rows, count), jnp.bfloat16),
            jax.ShapeDtypeStruct((len(masks), rows - shard_rows, count), jnp.float32),
        ),
        compiler_params=pltpu.CompilerParams(vmem_limit_bytes=SMALL_LIMIT),
        cost_estimate=pl.CostEstimate(
            flops=0, bytes_accessed=4 * len(masks) * rows * count, transcendentals=0
        ),
    )(*[pieces[mask] for mask in masks])


def rows_kernel(listed, per_shard, firsts, last_call, where_ref, tiles_ref, *refs):
    values_refs, (external_ref, held_ref, start_ref), (out_ref, total) = (
        refs[: len(firsts)],
        refs[len(firsts) : len(firsts) + 3],
        refs[len(firsts) + 3 :],
    )
    target = total if last_call else out_ref
    target[...] = start_ref[...].astype(jnp.float32)
    mine = where_ref[1] * per_shard + pl.program_id(0)

    for values_ref, first in zip(values_refs, firsts):

        def one_batch(b, carry, values_ref=values_ref, first=first):
            spots = [tiles_ref[(first + b) * listed + i] for i in range(listed)]
            owned = [s == mine for s in spots]

            @pl.when(functools.reduce(jnp.logical_or, owned))
            def _():
                values = values_ref[b]
                waves = None
                for i in range(listed):
                    orbital_rows = pl.ds(pl.multiple_of(spots[i] % per_shard * TILE, TILE), TILE)
                    part = jnp.dot(
                        values[:, i * TILE : (i + 1) * TILE],
                        held_ref[(spots[i] // per_shard) ^ where_ref[1], orbital_rows, :],
                        preferred_element_type=jnp.float32,
                    )
                    waves = part if waves is None else waves + part
                lifted = jnp.sum(waves * waves, axis=1, keepdims=True) * (3.0 / jnp.pi)
                root = jnp.where(lifted > 0.0, jnp.exp(jnp.log(lifted) * (1.0 / 3.0)), 0.0)
                lane = lax.broadcasted_iota(jnp.int32, external_ref.shape, 1)
                external = jnp.sum(
                    jnp.where(lane == first + b, external_ref[...], 0.0), axis=1, keepdims=True
                )
                potential = external - root
                weighted = (potential * values.astype(jnp.float32)).astype(jnp.bfloat16)
                place = sum(jnp.where(o, i, 0) for i, o in enumerate(owned))
                strip = lax.dot_general(
                    values_ref[b, :, pl.ds(pl.multiple_of(place * TILE, TILE), TILE)],
                    weighted,
                    (((0,), (0,)), ((), ())),
                    preferred_element_type=jnp.float32,
                )
                for j in range(listed):
                    columns = pl.ds(pl.multiple_of(spots[j] * TILE, TILE), TILE)
                    target[:, columns] += strip[:, j * TILE : (j + 1) * TILE]

            return carry

        lax.fori_loop(0, values_ref.shape[0], one_batch, 0)
    if last_call:
        out_ref[...] = total[...].astype(jnp.bfloat16)


def add_rows(where, tiles, pieces, firsts, external, held, start, shard_rows, last_call):
    batches, points, length = pieces[0].shape
    listed = length // TILE
    width = start.shape[1]
    groups = shard_rows // TILE
    first_call = start.shape[0] != shard_rows
    once = pl.Buffered(1)
    whole = pl.BlockSpec(
        (batches, points, length), lambda i, w, t: (0, 0, 0), pipeline_mode=once
    )
    rows = pl.BlockSpec((TILE, width), lambda i, w, t: (i, 0))
    return pl.pallas_call(
        functools.partial(rows_kernel, listed, groups, firsts, last_call),
        out_shape=jax.ShapeDtypeStruct((shard_rows, width), jnp.bfloat16 if last_call else jnp.float32),
        grid_spec=pltpu.PrefetchScalarGridSpec(
            num_scalar_prefetch=2,
            grid=(groups,),
            in_specs=[whole for _ in firsts]
            + [
                pl.BlockSpec(external.shape, lambda i, w, t: (0, 0)),
                pl.BlockSpec(held.shape, lambda i, w, t: (0, 0, 0), pipeline_mode=once),
                pl.BlockSpec((TILE, width), lambda i, w, t: (w[0] * groups + i, 0))
                if first_call
                else rows,
            ],
            out_specs=rows,
            scratch_shapes=[pltpu.VMEM((TILE, width) if last_call else (8, TILE), jnp.float32)],
        ),
        compiler_params=pltpu.CompilerParams(vmem_limit_bytes=LARGE_LIMIT if first_call else SMALL_LIMIT),
        cost_estimate=pl.CostEstimate(
            flops=len(firsts) * batches * 2 * points * length * TILE,
            bytes_accessed=2 * len(firsts) * batches * points * length + shard_rows * width * 8,
            transcendentals=0,
        ),
    )(where, tiles, *pieces, external, held, start)


def early_kernel(count, where_ref, *refs):
    out_ref = refs[-1]
    total = jnp.dot(refs[0][...], refs[count][...], preferred_element_type=jnp.float32)
    for i in range(1, count):
        total += jnp.dot(refs[i][...], refs[count + i][...], preferred_element_type=jnp.float32)
    if len(refs) > 2 * count + 1:
        total += refs[2 * count][0]
    out_ref[0] = total


def early_product(where, kinetic, pieces, masks, partners, limit, before=None):
    shard_rows, count = kinetic.shape[0] // (partners + 1), pieces[0].shape[1]
    whole = pl.BlockSpec((1, shard_rows, count), lambda s, w: (s, 0, 0))
    return pl.pallas_call(
        functools.partial(early_kernel, len(masks)),
        out_shape=jax.ShapeDtypeStruct((partners, shard_rows, count), jnp.float32),
        grid_spec=pltpu.PrefetchScalarGridSpec(
            num_scalar_prefetch=1,
            grid=(partners,),
            in_specs=[
                pl.BlockSpec(
                    (shard_rows, shard_rows),
                    lambda s, w, mask=mask: (w[0] ^ (s + 1), w[1] ^ mask),
                )
                for mask in masks
            ]
            + [pl.BlockSpec((shard_rows, count), lambda s, w: (0, 0)) for _ in masks]
            + [whole] * (before is not None),
            out_specs=whole,
        ),
        compiler_params=pltpu.CompilerParams(vmem_limit_bytes=limit),
        cost_estimate=pl.CostEstimate(
            flops=2 * partners * shard_rows * shard_rows * len(masks) * count,
            bytes_accessed=2 * partners * shard_rows * shard_rows * len(masks),
            transcendentals=0,
        ),
    )(where, *[kinetic] * len(masks), *pieces, *([] if before is None else [before]))


def late_kernel(count, where_ref, *refs):
    early_ref, out_ref = refs[-2:]
    total = early_ref[0]
    for i in range(count):
        total += jnp.dot(refs[i][...], refs[count + i][...], preferred_element_type=jnp.float32)
    out_ref[...] = total.astype(jnp.bfloat16)


def late_product(where, kinetic, pieces, masks, early, partner, limit):
    shard_rows, count = early.shape[1:]
    return pl.pallas_call(
        functools.partial(late_kernel, len(masks)),
        out_shape=jax.ShapeDtypeStruct((shard_rows, count), jnp.bfloat16),
        grid_spec=pltpu.PrefetchScalarGridSpec(
            num_scalar_prefetch=1,
            grid=(1,),
            in_specs=[
                pl.BlockSpec(
                    (shard_rows, shard_rows),
                    lambda s, w, mask=mask: (w[0] ^ partner, w[1] ^ mask),
                )
                for mask in masks
            ]
            + [pl.BlockSpec((shard_rows, count), lambda s, w: (0, 0)) for _ in masks]
            + [pl.BlockSpec((1, shard_rows, count), lambda s, w: (partner - 1, 0, 0))],
            out_specs=pl.BlockSpec((shard_rows, count), lambda s, w: (0, 0)),
        ),
        compiler_params=pltpu.CompilerParams(vmem_limit_bytes=limit),
        cost_estimate=pl.CostEstimate(
            flops=2 * shard_rows * shard_rows * len(masks) * count,
            bytes_accessed=2 * shard_rows * shard_rows * len(masks),
            transcendentals=0,
        ),
    )(where, *[kinetic] * len(masks), *pieces, early)


def own_kernel(count, where_ref, *refs):
    out_ref = refs[-1]
    total = jnp.dot(refs[0][...], refs[count][...], preferred_element_type=jnp.float32)
    for i in range(1, count):
        total += jnp.dot(refs[i][...], refs[count + i][...], preferred_element_type=jnp.float32)
    out_ref[...] = total


def own_product(where, own, pieces):
    shard_rows, count = own.shape[0], pieces[0].shape[1]
    masks = sorted(pieces)
    return pl.pallas_call(
        functools.partial(own_kernel, len(masks)),
        out_shape=jax.ShapeDtypeStruct((shard_rows, count), jnp.float32),
        grid_spec=pltpu.PrefetchScalarGridSpec(
            num_scalar_prefetch=1,
            grid=(1,),
            in_specs=[
                pl.BlockSpec((shard_rows, shard_rows), lambda s, w, mask=mask: (0, w[1] ^ mask))
                for mask in masks
            ]
            + [pl.BlockSpec((shard_rows, count), lambda s, w: (0, 0)) for _ in masks],
            out_specs=pl.BlockSpec((shard_rows, count), lambda s, w: (0, 0)),
        ),
        compiler_params=pltpu.CompilerParams(vmem_limit_bytes=SMALL_LIMIT),
        cost_estimate=pl.CostEstimate(
            flops=2 * shard_rows * shard_rows * len(masks) * count,
            bytes_accessed=2 * shard_rows * shard_rows * len(masks),
            transcendentals=0,
        ),
    )(where, *[own] * len(masks), *[pieces[mask] for mask in masks])


def body(grid_values, external, tiles, kinetic, orbitals):
    shard_rows, orbital_count = orbitals.shape
    batch_count, points, length = grid_values.shape
    row_count, col_count = lax.axis_size("row"), lax.axis_size("col")
    row = lax.axis_index("row")
    per_shard = shard_rows // TILE
    where = jnp.stack([lax.axis_index("col"), row]).astype(jnp.int32)
    _, depth = routes(row_count)
    masks = sorted(depth)
    soon = [mask for mask in masks if depth[mask] <= 1]
    middle = [mask for mask in masks if depth[mask] == 2]
    last = [mask for mask in masks if depth[mask] > 2]

    def first_products(pieces, limit=SMALL_LIMIT):
        return early_product(where, kinetic, [pieces[m] for m in soon], soon, col_count - 1, limit)

    def second_products(pieces, early, limit=SMALL_LIMIT):
        return early_product(
            where, kinetic, [pieces[m] for m in middle], middle, col_count - 1, limit, early
        )

    def sums(pieces, early, limit=SMALL_LIMIT):
        return [
            late_product(where, kinetic, [pieces[m] for m in last], last, early, partner, limit)
            for partner in range(col_count - 1, 0, -1)
        ]

    def send(parts):
        return [swap(part, "col", len(parts) - i) for i, part in enumerate(parts)]

    orbital_pieces = spread_out(noted(orbitals, external, tiles))
    held, notes = stacked(orbital_pieces, shard_rows)
    notes = notes.reshape(row_count, -1)
    group_external = (
        notes[:, : external.size]
        + notes[:, external.size : 2 * external.size]
        + notes[:, 2 * external.size : 3 * external.size]
    )
    group_external = group_external.reshape(-1, points).T
    group_tiles = notes[:, 3 * external.size : 3 * external.size + tiles.size]
    group_tiles = group_tiles.astype(jnp.int32).reshape(-1)

    half = batch_count // 2

    def rows_of(chosen, start, last_call):
        return add_rows(
            where,
            group_tiles,
            [value_pieces[part][mask] for mask, part in chosen],
            [mask * batch_count + part * half for mask, part in chosen],
            group_external,
            held,
            start,
            shard_rows,
            last_call,
        )

    def finish(pieces, arrived, vectors):
        reduced = own_product(where, own, pieces)
        for part in arrived:
            reduced = reduced + part.astype(jnp.float32)
        return reduced / spread - center / spread * vectors.astype(jnp.float32)

    value_pieces = [{0: grid_values[:half]}, {0: grid_values[half:]}]
    early = first_products(orbital_pieces, LARGE_LIMIT)
    early = second_products(orbital_pieces, early, LARGE_LIMIT)
    plans = turns(row_count)
    taken, total = [], kinetic

    def arrived_values():
        return [(m, p) for p in range(2) for m in sorted(value_pieces[p])]

    for turn in range(len(plans[0])):
        fresh = [which for which in arrived_values() if which not in taken]
        if turn == 0:
            orbital_pieces = hop(value_pieces[0], plans[0][turn], orbital_pieces)
            orbital_pieces = hop(value_pieces[1], plans[1][turn], orbital_pieces)
            continue
        value_pieces[1], early = hop(value_pieces[0], plans[0][turn], (value_pieces[1], early))
        if turn == 1:
            early = hop(value_pieces[1], plans[1][turn], early)
            early = sums(orbital_pieces, early, LARGE_LIMIT)
        else:
            total = hop(value_pieces[1], plans[1][turn], total)
        total = rows_of(fresh, total, False)
        taken = taken + fresh
    arrived = send(early)
    rest = [which for which in arrived_values() if which not in taken]
    own = rows_of(rest, total, True)
    first_term = finish(orbital_pieces, arrived, orbitals).astype(jnp.bfloat16)
    first_pieces, early = spread_out(first_term, first_products)
    second_term = (
        2.0 * finish(first_pieces, send(sums(first_pieces, second_products(first_pieces, early))), first_term)
        - orbitals.astype(jnp.float32)
    ).astype(jnp.bfloat16)
    second_pieces, early = spread_out(second_term, first_products)
    return 2.0 * finish(second_pieces, send(sums(second_pieces, second_products(second_pieces, early))), second_term) - first_term.astype(
        jnp.float32
    )


def solution(mesh):
    return jax.shard_map(
        body,
        mesh=mesh,
        in_specs=(
            P(("row", "col"), None, None),
            P(("row", "col"), None),
            P(("row", "col"), None),
            P("row", "col"),
            P(("row", "col"), None),
        ),
        out_specs=P(("row", "col"), None),
        check_vma=False,
    )
```

```python
import functools

import jax
import jax.numpy as jnp
from jax import lax
from jax.experimental import pallas as pl
from jax.experimental.pallas import tpu as pltpu
from jax.sharding import PartitionSpec as P

TILE = 128
SMALL_LIMIT = 18 * 2**20
LARGE_LIMIT = 36 * 2**20
center = 1.0
spread = 2.5


def routes(count):
    found, depth = [], {0: 0}

    def add(mask, source, step):
        depth[mask] = depth[source] + 1
        found.append((mask, source, step))

    for k in sorted(range(1, count // 2), key=lambda k: (k & (k + 1)) != 0):
        full = (1 << k.bit_length()) - 1
        add(2 * k, 0 if k == full else 2 * full, 2 * k if k == full else 2 * (full ^ k))
    if count > 1:
        add(1, 0, 1)
    for k in sorted(range(1, count // 2), key=lambda k: (k & (k + 1)) != 0):
        full = (1 << k.bit_length()) - 1
        add(2 * k + 1, 2 * k if k == full else 2 * full + 1, 1 if k == full else 2 * (full ^ k))
    return sorted(found, key=lambda route: depth[route[0]]), depth


def swap(array, axis, mask):
    return lax.ppermute(array, axis, [(i, i ^ mask) for i in range(lax.axis_size(axis))])


def spread_out(array, between=None):
    order, depth = routes(lax.axis_size("row"))
    pieces, result = {0: array}, None
    for mask, source, step in order:
        outgoing = pieces[source]
        if between is not None and depth[mask] > 2:
            if result is None:
                result = between(pieces)
            outgoing, result = lax.optimization_barrier((outgoing, result))
        pieces[mask] = swap(outgoing, "row", step)
    if between is None:
        return pieces
    return pieces, between(pieces) if result is None else result


def hop(pieces, chosen, after):
    held, after = lax.optimization_barrier((dict(pieces), after))
    pieces.update(held)
    for mask, source, step in chosen:
        pieces[mask] = swap(pieces[source], "row", step)
    return after


def turns(count):
    order, _ = routes(count)
    near = [route for route in order if route[0] % 2 == 0 and route[1] == 0]
    side = [route for route in order if route[0] == 1]
    near_side = [(mask + 1, mask, 1) for mask, _, _ in near]
    far = [route for route in order if route[0] % 2 == 0 and route[1] != 0]
    far_side = [route for route in order if route[0] - 1 in [mask for mask, _, _ in far]]
    last_side = [(mask + 1, mask, 1) for mask, _, _ in far]
    return [near + side, near_side, far, far_side], [side, near, near_side + far, last_side]


def noted(orbitals, external, tiles):
    parts, rest = [], external
    for _ in range(3):
        part = lax.reduce_precision(rest, exponent_bits=8, mantissa_bits=7)
        parts.append(part.reshape(-1))
        rest = rest - part
    flat = jnp.concatenate(parts + [tiles.astype(jnp.float32).reshape(-1)])
    count = orbitals.shape[1]
    flat = jnp.pad(flat, (0, -flat.size % (16 * count))).astype(jnp.bfloat16)
    return jnp.concatenate([orbitals, flat.reshape(-1, count)], axis=0)


def stack_kernel(count, *refs):
    held_ref, notes_ref = refs[count:]
    rows = held_ref.shape[1]
    for i in range(count):
        held_ref[i] = refs[i][:rows]
        notes_ref[i] = refs[i][rows:].astype(jnp.float32)


def stacked(pieces, shard_rows):
    masks = sorted(pieces)
    rows, count = pieces[0].shape
    return pl.pallas_call(
        functools.partial(stack_kernel, len(masks)),
        out_shape=(
            jax.ShapeDtypeStruct((len(masks), shard_rows, count), jnp.bfloat16),
            jax.ShapeDtypeStruct((len(masks), rows - shard_rows, count), jnp.float32),
        ),
        compiler_params=pltpu.CompilerParams(vmem_limit_bytes=SMALL_LIMIT),
        cost_estimate=pl.CostEstimate(
            flops=0, bytes_accessed=4 * len(masks) * rows * count, transcendentals=0
        ),
    )(*[pieces[mask] for mask in masks])


def rows_kernel(listed, per_shard, firsts, last_call, where_ref, tiles_ref, *refs):
    values_refs, (external_ref, held_ref, start_ref), (out_ref, total) = (
        refs[: len(firsts)],
        refs[len(firsts) : len(firsts) + 3],
        refs[len(firsts) + 3 :],
    )
    target = total if last_call else out_ref
    target[...] = start_ref[...].astype(jnp.float32)
    mine = where_ref[1] * per_shard + pl.program_id(0)

    for values_ref, first in zip(values_refs, firsts):

        def one_batch(b, carry, values_ref=values_ref, first=first):
            spots = [tiles_ref[(first + b) * listed + i] for i in range(listed)]
            owned = [s == mine for s in spots]

            @pl.when(functools.reduce(jnp.logical_or, owned))
            def _():
                values = values_ref[b]
                waves = None
                for i in range(listed):
                    orbital_rows = pl.ds(pl.multiple_of(spots[i] % per_shard * TILE, TILE), TILE)
                    part = jnp.dot(
                        values[:, i * TILE : (i + 1) * TILE],
                        held_ref[(spots[i] // per_shard) ^ where_ref[1], orbital_rows, :],
                        preferred_element_type=jnp.float32,
                    )
                    waves = part if waves is None else waves + part
                lifted = jnp.sum(waves * waves, axis=1, keepdims=True) * (3.0 / jnp.pi)
                root = jnp.where(lifted > 0.0, jnp.exp(jnp.log(lifted) * (1.0 / 3.0)), 0.0)
                lane = lax.broadcasted_iota(jnp.int32, external_ref.shape, 1)
                external = jnp.sum(
                    jnp.where(lane == first + b, external_ref[...], 0.0), axis=1, keepdims=True
                )
                potential = external - root
                weighted = (potential * values.astype(jnp.float32)).astype(jnp.bfloat16)
                place = sum(jnp.where(o, i, 0) for i, o in enumerate(owned))
                strip = lax.dot_general(
                    values_ref[b, :, pl.ds(pl.multiple_of(place * TILE, TILE), TILE)],
                    weighted,
                    (((0,), (0,)), ((), ())),
                    preferred_element_type=jnp.float32,
                )
                for j in range(listed):
                    columns = pl.ds(pl.multiple_of(spots[j] * TILE, TILE), TILE)
                    target[:, columns] += strip[:, j * TILE : (j + 1) * TILE]

            return carry

        lax.fori_loop(0, values_ref.shape[0], one_batch, 0)
    if last_call:
        out_ref[...] = total[...].astype(jnp.bfloat16)


def add_rows(where, tiles, pieces, firsts, external, held, start, shard_rows, last_call):
    batches, points, length = pieces[0].shape
    listed = length // TILE
    width = start.shape[1]
    groups = shard_rows // TILE
    first_call = start.shape[0] != shard_rows
    once = pl.Buffered(1)
    whole = pl.BlockSpec(
        (batches, points, length), lambda i, w, t: (0, 0, 0), pipeline_mode=once
    )
    rows = pl.BlockSpec((TILE, width), lambda i, w, t: (i, 0))
    return pl.pallas_call(
        functools.partial(rows_kernel, listed, groups, firsts, last_call),
        out_shape=jax.ShapeDtypeStruct((shard_rows, width), jnp.bfloat16 if last_call else jnp.float32),
        grid_spec=pltpu.PrefetchScalarGridSpec(
            num_scalar_prefetch=2,
            grid=(groups,),
            in_specs=[whole for _ in firsts]
            + [
                pl.BlockSpec(external.shape, lambda i, w, t: (0, 0)),
                pl.BlockSpec(held.shape, lambda i, w, t: (0, 0, 0), pipeline_mode=once),
                pl.BlockSpec((TILE, width), lambda i, w, t: (w[0] * groups + i, 0))
                if first_call
                else rows,
            ],
            out_specs=rows,
            scratch_shapes=[pltpu.VMEM((TILE, width) if last_call else (8, TILE), jnp.float32)],
        ),
        compiler_params=pltpu.CompilerParams(vmem_limit_bytes=LARGE_LIMIT if first_call else SMALL_LIMIT),
        cost_estimate=pl.CostEstimate(
            flops=len(firsts) * batches * 2 * points * length * TILE,
            bytes_accessed=2 * len(firsts) * batches * points * length + shard_rows * width * 8,
            transcendentals=0,
        ),
    )(where, tiles, *pieces, external, held, start)


def early_kernel(count, where_ref, *refs):
    out_ref = refs[-1]
    total = jnp.dot(refs[0][...], refs[count][...], preferred_element_type=jnp.float32)
    for i in range(1, count):
        total += jnp.dot(refs[i][...], refs[count + i][...], preferred_element_type=jnp.float32)
    if len(refs) > 2 * count + 1:
        total += refs[2 * count][0]
    out_ref[0] = total


def early_product(where, kinetic, pieces, masks, partners, limit, before=None):
    shard_rows, count = kinetic.shape[0] // (partners + 1), pieces[0].shape[1]
    whole = pl.BlockSpec((1, shard_rows, count), lambda s, w: (s, 0, 0))
    return pl.pallas_call(
        functools.partial(early_kernel, len(masks)),
        out_shape=jax.ShapeDtypeStruct((partners, shard_rows, count), jnp.float32),
        grid_spec=pltpu.PrefetchScalarGridSpec(
            num_scalar_prefetch=1,
            grid=(partners,),
            in_specs=[
                pl.BlockSpec(
                    (shard_rows, shard_rows),
                    lambda s, w, mask=mask: (w[0] ^ (s + 1), w[1] ^ mask),
                )
                for mask in masks
            ]
            + [pl.BlockSpec((shard_rows, count), lambda s, w: (0, 0)) for _ in masks]
            + [whole] * (before is not None),
            out_specs=whole,
        ),
        compiler_params=pltpu.CompilerParams(vmem_limit_bytes=limit),
        cost_estimate=pl.CostEstimate(
            flops=2 * partners * shard_rows * shard_rows * len(masks) * count,
            bytes_accessed=2 * partners * shard_rows * shard_rows * len(masks),
            transcendentals=0,
        ),
    )(where, *[kinetic] * len(masks), *pieces, *([] if before is None else [before]))


def late_kernel(count, where_ref, *refs):
    early_ref, out_ref = refs[-2:]
    total = early_ref[0]
    for i in range(count):
        total += jnp.dot(refs[i][...], refs[count + i][...], preferred_element_type=jnp.float32)
    out_ref[...] = total.astype(jnp.bfloat16)


def late_product(where, kinetic, pieces, masks, early, partner, limit):
    shard_rows, count = early.shape[1:]
    return pl.pallas_call(
        functools.partial(late_kernel, len(masks)),
        out_shape=jax.ShapeDtypeStruct((shard_rows, count), jnp.bfloat16),
        grid_spec=pltpu.PrefetchScalarGridSpec(
            num_scalar_prefetch=1,
            grid=(1,),
            in_specs=[
                pl.BlockSpec(
                    (shard_rows, shard_rows),
                    lambda s, w, mask=mask: (w[0] ^ partner, w[1] ^ mask),
                )
                for mask in masks
            ]
            + [pl.BlockSpec((shard_rows, count), lambda s, w: (0, 0)) for _ in masks]
            + [pl.BlockSpec((1, shard_rows, count), lambda s, w: (partner - 1, 0, 0))],
            out_specs=pl.BlockSpec((shard_rows, count), lambda s, w: (0, 0)),
        ),
        compiler_params=pltpu.CompilerParams(vmem_limit_bytes=limit),
        cost_estimate=pl.CostEstimate(
            flops=2 * shard_rows * shard_rows * len(masks) * count,
            bytes_accessed=2 * shard_rows * shard_rows * len(masks),
            transcendentals=0,
        ),
    )(where, *[kinetic] * len(masks), *pieces, early)


def own_kernel(count, where_ref, *refs):
    out_ref = refs[-1]
    total = jnp.dot(refs[0][...], refs[count][...], preferred_element_type=jnp.float32)
    for i in range(1, count):
        total += jnp.dot(refs[i][...], refs[count + i][...], preferred_element_type=jnp.float32)
    out_ref[...] = total


def own_product(where, own, pieces):
    shard_rows, count = own.shape[0], pieces[0].shape[1]
    masks = sorted(pieces)
    return pl.pallas_call(
        functools.partial(own_kernel, len(masks)),
        out_shape=jax.ShapeDtypeStruct((shard_rows, count), jnp.float32),
        grid_spec=pltpu.PrefetchScalarGridSpec(
            num_scalar_prefetch=1,
            grid=(1,),
            in_specs=[
                pl.BlockSpec((shard_rows, shard_rows), lambda s, w, mask=mask: (0, w[1] ^ mask))
                for mask in masks
            ]
            + [pl.BlockSpec((shard_rows, count), lambda s, w: (0, 0)) for _ in masks],
            out_specs=pl.BlockSpec((shard_rows, count), lambda s, w: (0, 0)),
        ),
        compiler_params=pltpu.CompilerParams(vmem_limit_bytes=SMALL_LIMIT),
        cost_estimate=pl.CostEstimate(
            flops=2 * shard_rows * shard_rows * len(masks) * count,
            bytes_accessed=2 * shard_rows * shard_rows * len(masks),
            transcendentals=0,
        ),
    )(where, *[own] * len(masks), *[pieces[mask] for mask in masks])


def body(grid_values, external, tiles, kinetic, orbitals):
    shard_rows, orbital_count = orbitals.shape
    batch_count, points, length = grid_values.shape
    row_count, col_count = lax.axis_size("row"), lax.axis_size("col")
    row = lax.axis_index("row")
    per_shard = shard_rows // TILE
    where = jnp.stack([lax.axis_index("col"), row]).astype(jnp.int32)
    _, depth = routes(row_count)
    masks = sorted(depth)
    soon = [mask for mask in masks if depth[mask] <= 1]
    middle = [mask for mask in masks if depth[mask] == 2]
    last = [mask for mask in masks if depth[mask] > 2]

    def first_products(pieces, limit=SMALL_LIMIT):
        return early_product(where, kinetic, [pieces[m] for m in soon], soon, col_count - 1, limit)

    def second_products(pieces, early, limit=SMALL_LIMIT):
        return early_product(
            where, kinetic, [pieces[m] for m in middle], middle, col_count - 1, limit, early
        )

    def sums(pieces, early, limit=SMALL_LIMIT):
        return [
            late_product(where, kinetic, [pieces[m] for m in last], last, early, partner, limit)
            for partner in range(col_count - 1, 0, -1)
        ]

    def send(parts):
        return [swap(part, "col", len(parts) - i) for i, part in enumerate(parts)]

    orbital_pieces = spread_out(noted(orbitals, external, tiles))
    held, notes = stacked(orbital_pieces, shard_rows)
    notes = notes.reshape(row_count, -1)
    group_external = (
        notes[:, : external.size]
        + notes[:, external.size : 2 * external.size]
        + notes[:, 2 * external.size : 3 * external.size]
    )
    group_external = group_external.reshape(-1, points).T
    group_tiles = notes[:, 3 * external.size : 3 * external.size + tiles.size]
    group_tiles = group_tiles.astype(jnp.int32).reshape(-1)

    half = batch_count // 2

    def rows_of(chosen, start, last_call):
        return add_rows(
            where,
            group_tiles,
            [value_pieces[part][mask] for mask, part in chosen],
            [mask * batch_count + part * half for mask, part in chosen],
            group_external,
            held,
            start,
            shard_rows,
            last_call,
        )

    def finish(pieces, arrived, vectors):
        reduced = own_product(where, own, pieces)
        for part in arrived:
            reduced = reduced + part.astype(jnp.float32)
        return reduced / spread - center / spread * vectors.astype(jnp.float32)

    value_pieces = [{0: grid_values[:half]}, {0: grid_values[half:]}]
    early = first_products(orbital_pieces, LARGE_LIMIT)
    early = second_products(orbital_pieces, early, LARGE_LIMIT)
    plans = turns(row_count)
    taken, total = [], kinetic

    def arrived_values():
        return [(m, p) for p in range(2) for m in sorted(value_pieces[p])]

    for turn in range(len(plans[0])):
        fresh = [which for which in arrived_values() if which not in taken]
        if turn == 0:
            orbital_pieces = hop(value_pieces[0], plans[0][turn], orbital_pieces)
            orbital_pieces = hop(value_pieces[1], plans[1][turn], orbital_pieces)
            continue
        value_pieces[1], early = hop(value_pieces[0], plans[0][turn], (value_pieces[1], early))
        if turn == 1:
            early = hop(value_pieces[1], plans[1][turn], early)
            early = sums(orbital_pieces, early, LARGE_LIMIT)
        else:
            total = hop(value_pieces[1], plans[1][turn], total)
        total = rows_of(fresh, total, False)
        taken = taken + fresh
    arrived = send(early)
    rest = [which for which in arrived_values() if which not in taken]
    own = rows_of(rest, total, True)
    first_term = finish(orbital_pieces, arrived, orbitals).astype(jnp.bfloat16)
    first_pieces, early = spread_out(first_term, first_products)
    second_term = (
        2.0 * finish(first_pieces, send(sums(first_pieces, second_products(first_pieces, early))), first_term)
        - orbitals.astype(jnp.float32)
    ).astype(jnp.bfloat16)
    second_pieces, early = spread_out(second_term, first_products)
    return 2.0 * finish(second_pieces, send(sums(second_pieces, second_products(second_pieces, early))), second_term) - first_term.astype(
        jnp.float32
    )


def solution(mesh):
    return jax.shard_map(
        body,
        mesh=mesh,
        in_specs=(
            P(("row", "col"), None, None),
            P(("row", "col"), None),
            P(("row", "col"), None),
            P("row", "col"),
            P(("row", "col"), None),
        ),
        out_specs=P(("row", "col"), None),
        check_vma=False,
    )
```
